256 devices in a mesh: row: 16 (over z, core), col: 16 (over x, y).
Axes of the slice: x: 4, y: 4, z: 8, core: 2. Of those that a mesh axis runs over, the one named last changes fastest.
Arguments:
- panels: bfloat16 [2, 16384, 512], P(None, 'row'), may hold values from -2 to 2
- row_pattern: int32 [2, 128], replicated, may hold values from 0 to 1, as said below
- coupling: bfloat16 [512, 512], P('row'), may hold values from -0.3125 to 0.3125
- inverse_factors: bfloat16 [2, 512, 512], replicated, as said below
- trailing: float32 [16384, 16384], P('row', 'col'), may hold values from -6 to 6
Outputs:
- factor: bfloat16 [2, 16384, 512], P(None, 'row')
- updated: float32 [16384, 16384], P('row', 'col')
The draws below stay inside these ranges and needn't reach their ends.
Inputs may be any that keep to these rules, and one draw needn't show every extreme that they name: `row_pattern`: in each panel, the 8 entries of every aligned block (the tile rows of one index of row) hold 1 to 3 ones, and some block of each panel holds exactly 3. `inverse_factors`: each block is lower triangular with a positive diagonal.
All inputs are finite; a program needn't handle non-finite values.
Results may differ from the reference program's by a relative error of at most 0.0023.
Values may be sent and summed in bfloat16 or wider, within the bound.
A program may use at most 64 MiB of HBM per device.

```python
import math
import jax
import jax.numpy as jnp
from jax import lax

W = 512
BS = 128
TR_DEV = 8
PMAX = 3
MT = 128
ROWS = 16384
N_ROW = 16
N_COL = 16


def draw_row_pattern(key, part):
    key = jax.random.fold_in(key, 11)
    count_key, fill_key, score_key = jax.random.split(key, 3)
    blocks = MT // TR_DEV
    counts = jax.random.randint(count_key, (2, blocks), 1, PMAX + 1)
    fullest = jax.random.randint(fill_key, (2, 1), 0, blocks)
    counts = jnp.where(jnp.arange(blocks)[None, :] == fullest, PMAX, counts)
    scores = jax.random.randint(score_key, (2, blocks, TR_DEV), 0, 1 << 20) * TR_DEV + jnp.arange(TR_DEV)
    ranks = jnp.argsort(jnp.argsort(scores, axis=2), axis=2)
    return (ranks < counts[:, :, None]).astype(jnp.int32).reshape(2, MT)


def draw_inverse_factors(key, part):
    key = jax.random.fold_in(key, 12)
    diag_key, off_key = jax.random.split(key, 2)
    diagonal = jax.random.uniform(diag_key, (2, W), minval=0.8, maxval=1.25)
    off_diagonal = jax.random.normal(off_key, (2, W, W)) * (0.6 / math.sqrt(W))
    lower = jnp.tril(off_diagonal, -1) + diagonal[:, :, None] * jnp.eye(W, dtype=jnp.float32)
    return lower.astype(jnp.bfloat16)


def level_of(rng, extent, cuts, least, high):
    loudness, own = 1.0, jax.random.fold_in(rng, 6)
    for axis_at, blocks in cuts:
        heights = jnp.exp(jax.random.uniform(jax.random.fold_in(own, axis_at), (blocks,), jnp.float32, least / len(cuts), high / len(cuts)))
        loudness = loudness * jnp.repeat(heights, extent[axis_at] // blocks).reshape([-1 if axis == axis_at else 1 for axis in range(len(extent))])
    return loudness


def centred(rng, dims, width, most, shards=(), kind=jnp.bfloat16):
    entries = jax.random.normal(rng, dims, jnp.float32) * width
    if len(shards) > 0:
        entries = level_of(rng, dims, shards, -0.22, 0.18) * entries
    return jnp.clip(entries, min=-most, max=most).astype(kind)


def setup_inputs(seed: int = 0) -> dict:
    streams_of = jax.random.split(jax.random.key(seed), 6)
    return {
        "panels": centred(streams_of[0], (2, ROWS, W), 0.15, 2.0, ((1, 16),)),
        "row_pattern": draw_row_pattern(jax.random.fold_in(streams_of[5], 71), 0),
        "coupling": centred(streams_of[2], (W, W), 0.02, 0.3125, ((0, 16),)),
        "inverse_factors": draw_inverse_factors(jax.random.fold_in(streams_of[5], 71), 0),
        "trailing": centred(streams_of[4], (ROWS, ROWS), 1.0, 6.0, ((0, 16), (1, 16)), jnp.float32),
    }


def reference(panels, row_pattern, coupling, inverse_factors, trailing):
    present = jnp.repeat(row_pattern.astype(jnp.float32), BS, axis=1)[:, :, None]
    first = (jnp.dot(panels[0], inverse_factors[0].T, preferred_element_type=jnp.float32) * present[0]).astype(jnp.bfloat16)
    coupled = jnp.dot(coupling, inverse_factors[0].T, preferred_element_type=jnp.float32).astype(jnp.bfloat16)
    second_input = panels[1].astype(jnp.float32) - jnp.dot(first, coupled.T, preferred_element_type=jnp.float32)
    second = (jnp.dot(second_input, inverse_factors[1].astype(jnp.float32).T, precision=lax.Precision.HIGHEST) * present[1]).astype(jnp.bfloat16)
    factor = jnp.stack((first, second))
    row_side = jnp.concatenate((first, second), axis=1)
    global_side = row_side.reshape(N_ROW, TR_DEV, BS, 2 * W).transpose(1, 0, 2, 3).reshape(MT, BS, 2 * W)
    column_side = global_side.reshape(MT // N_COL, N_COL, BS, 2 * W).transpose(1, 0, 2, 3).reshape(ROWS, 2 * W)
    update = jnp.dot(row_side.astype(jnp.float32), column_side.astype(jnp.float32).T, precision=lax.Precision.HIGHEST)
    return factor, trailing - update
```

```python
import jax
import jax.numpy as jnp
from jax import lax
from jax.experimental import pallas as pl
from jax.experimental.pallas import tpu as pltpu
from jax.sharding import PartitionSpec as P

W = 512
BS = 128
TR = 8
PMAX = 3
NZ = 8
NP = 16
MESH = pl.DeviceIdType.MESH
BF = jnp.bfloat16
F32 = jnp.float32


def dot_t(a, b):
    return lax.dot_general(a, b, (((1,), (1,)), ((), ())), preferred_element_type=F32)


def places(pattern, panel, block):
    tiles = [jnp.int32(0)] * PMAX
    ranks = []
    count = jnp.int32(0)
    for i in range(TR):
        bit = pattern[panel, block * TR + i]
        for j in range(min(i + 1, PMAX)):
            tiles[j] = jnp.where((bit == 1) & (count == j), i, tiles[j])
        ranks.append(jnp.where(bit == 1, count, PMAX))
        count = count + bit
    return tiles, ranks, count


def pick(ranks, tile):
    rank = jnp.int32(PMAX)
    for i in range(TR):
        rank = jnp.where(tile == i, ranks[i], rank)
    return rank


def second_of(panel_one, gathered_first, coupled, inverse):
    held = panel_one.astype(F32) - dot_t(gathered_first, coupled)
    high = held.astype(BF)
    low = (held - high.astype(F32)).astype(BF)
    return dot_t(high, inverse) + dot_t(low, inverse)


def exchange(
    pattern_hbm, panels_hbm, coupling_hbm, inverse_hbm, trailing_hbm,
    own_ref, other_ref, trail_ref,
    pattern, cand, sendbuf, panv, inv, coup, coupled, dland, first, pick_buf,
    local_sem, bsend, brecv, fsend, frecv, dsend, drecv, gsend, grecv, osend,
):
    r = lax.axis_index("row")
    c = lax.axis_index("col")
    z, k = r // 2, r % 2
    zc = c // 2
    sibling = (z * 2 + 1 - k, c)
    half = c % 2

    def plane(i):
        return lax.rem(z + 1 + i, NZ)

    barrier = pltpu.get_barrier_semaphore()

    def greet(device):
        pl.semaphore_signal(barrier, inc=1, device_id=device, device_id_type=MESH)

    greet(sibling)
    for i in range(NZ - 1):
        greet((plane(i) * 2 + k, c))

    @pl.when(z != zc)
    def _():
        for i in range(NP // 2):
            greet((c, 2 * i + k))

    local = [
        pltpu.make_async_copy(pattern_hbm, pattern, local_sem.at[0]),
        pltpu.make_async_copy(
            panels_hbm.at[:, :, pl.ds(pl.multiple_of(16 * (c // 2), 16), 16), pl.ds(pl.multiple_of(256 * half, 256), 256)],
            cand, local_sem.at[1]),
        pltpu.make_async_copy(coupling_hbm, coup.at[pl.ds(pl.multiple_of(32 * r, 32), 32)], local_sem.at[2]),
        pltpu.make_async_copy(panels_hbm, panv, local_sem.at[3]),
        pltpu.make_async_copy(inverse_hbm, inv, local_sem.at[4]),
        pltpu.make_async_copy(trailing_hbm, trail_ref, local_sem.at[5]),
    ]
    for copy in local:
        copy.start()
    pl.semaphore_wait(barrier, 2 * NZ - 1)

    mine = coup.at[pl.ds(pl.multiple_of(32 * r, 32), 32)]
    local[2].wait()
    shard_copies = []
    for i in range(NZ - 1):
        copy = pltpu.make_async_remote_copy(
            src_ref=mine, dst_ref=mine, send_sem=bsend.at[i], recv_sem=brecv.at[NZ - 2 - i],
            device_id=(plane(i) * 2 + k, c), device_id_type=MESH)
        copy.start()
        shard_copies.append(copy)
    own_forward = pltpu.make_async_remote_copy(
        src_ref=mine, dst_ref=mine, send_sem=fsend.at[NZ - 1], recv_sem=frecv.at[NZ - 1],
        device_id=sibling, device_id_type=MESH)
    own_forward.start()

    local[0].wait()
    local[1].wait()
    own_places = [places(pattern, q, r) for q in range(2)]
    for q in range(2):
        tiles, _, count = own_places[q]
        for j in range(PMAX):
            value = cand[q, tiles[j]]
            sendbuf[q, j] = jnp.where(count > j, value, jnp.zeros_like(value))
    piece_rows = pl.ds(pl.multiple_of(16 * (c // 2), 16), 16)
    piece_cols = pl.ds(pl.multiple_of(256 * half, 256), 256)
    piece_copies = []
    for i in range(NZ - 1):
        copy = pltpu.make_async_remote_copy(
            src_ref=sendbuf, dst_ref=dland.at[:, :, piece_rows, piece_cols],
            send_sem=dsend.at[i], recv_sem=drecv.at[c // 2],
            device_id=(plane(i) * 2 + half, r), device_id_type=MESH)
        copy.start()
        piece_copies.append(copy)

    local[3].wait()
    for q in range(2):
        tiles, _, count = own_places[q]
        for j in range(PMAX):
            value = panv[q, tiles[j]]
            pick_buf[q, j] = jnp.where(count > j, value, jnp.zeros_like(value))

    @pl.when(r == c)
    def _():
        dland[...] = pick_buf[...]
        pltpu.make_async_remote_copy(
            src_ref=pick_buf, dst_ref=dland, send_sem=osend.at[0], recv_sem=osend.at[1],
            device_id=sibling, device_id_type=MESH).start()

    local[4].wait()
    first[PMAX] = jnp.zeros((BS, W), BF)
    own_first = dot_t(pick_buf[0].reshape(PMAX * BS, W), inv[0]).astype(BF).reshape(PMAX, BS, W)
    first[:PMAX] = own_first
    own_ref[0] = own_first

    for i in range(NZ - 1):
        shard_copies[NZ - 2 - i].wait_recv()
        there = coup.at[pl.ds(pl.multiple_of(32 * (plane(i) * 2 + k), 32), 32)]
        pltpu.make_async_remote_copy(
            src_ref=there, dst_ref=there, send_sem=fsend.at[i], recv_sem=frecv.at[i],
            device_id=sibling, device_id_type=MESH).start()

    def piece_at(i):
        return dland.at[:, :, pl.ds(16 * i, 16), pl.ds(pl.multiple_of(256 * k, 256), 256)]

    def piece_forward(i):
        return pltpu.make_async_remote_copy(
            src_ref=piece_at(i), dst_ref=piece_at(i), send_sem=gsend.at[i], recv_sem=grecv.at[i],
            device_id=sibling, device_id_type=MESH)

    @pl.when(z != zc)
    def _():
        for i in range(NP // 2):
            pltpu.make_async_remote_copy(
                src_ref=sendbuf, dst_ref=piece_at(i), send_sem=dsend.at[0], recv_sem=drecv.at[i],
                device_id=sibling, device_id_type=MESH).wait_recv()
            piece_forward(i).start()

    for i in range(NZ):
        there = coup.at[pl.ds(pl.multiple_of(32 * (plane(i) * 2 + 1 - k), 32), 32)]
        pltpu.make_async_remote_copy(
            src_ref=there, dst_ref=there, send_sem=fsend.at[i], recv_sem=frecv.at[i],
            device_id=sibling, device_id_type=MESH).wait_recv()
    coupled[...] = dot_t(coup[...], inv[0]).astype(BF)

    def masked_gather(of_places):
        count = of_places[1][2]
        parts = []
        for j in range(PMAX):
            value = first[pick(of_places[0][1], of_places[1][0][j])]
            parts.append(jnp.where(count > j, value, jnp.zeros_like(value)))
        return jnp.concatenate(parts, axis=0)

    own_ref[1] = second_of(
        pick_buf[1].reshape(PMAX * BS, W), masked_gather(own_places), coupled[...], inv[1]
    ).astype(BF).reshape(PMAX, BS, W)

    @pl.when(z != zc)
    def _():
        for i in range(NP // 2):
            pltpu.make_async_remote_copy(
                src_ref=sendbuf, dst_ref=dland.at[:, :, pl.ds(16 * i, 16), pl.ds(pl.multiple_of(256 * (1 - k), 256), 256)],
                send_sem=gsend.at[i], recv_sem=grecv.at[i],
                device_id=sibling, device_id_type=MESH).wait_recv()

    whole = pltpu.make_async_remote_copy(
        src_ref=pick_buf, dst_ref=dland, send_sem=osend.at[0], recv_sem=osend.at[1],
        device_id=sibling, device_id_type=MESH)

    @pl.when((z == zc) & (r != c))
    def _():
        whole.wait_recv()

    other_places = [places(pattern, q, c) for q in range(2)]
    other_first = dot_t(dland[0].reshape(PMAX * BS, W), inv[0]).astype(BF).reshape(PMAX, BS, W)
    first[:PMAX] = other_first
    other_ref[0] = other_first
    other_ref[1] = second_of(
        dland[1].reshape(PMAX * BS, W), masked_gather(other_places), coupled[...], inv[1]
    ).astype(BF).reshape(PMAX, BS, W)

    local[5].wait()
    for copy in shard_copies + piece_copies:
        copy.wait_send()
    own_forward.wait_send()
    for i in range(NZ - 1):
        there = coup.at[pl.ds(pl.multiple_of(32 * (plane(i) * 2 + k), 32), 32)]
        pltpu.make_async_remote_copy(
            src_ref=there, dst_ref=there, send_sem=fsend.at[i], recv_sem=frecv.at[i],
            device_id=sibling, device_id_type=MESH).wait_send()

    @pl.when(z != zc)
    def _():
        for i in range(NP // 2):
            piece_forward(i).wait_send()

    @pl.when(r == c)
    def _():
        whole.wait_send()


def finish(pattern_hbm, own, other, trail, factor_hbm, updated_hbm, pattern, zeros, products, strip, sem):
    r = lax.axis_index("row")
    c = lax.axis_index("col")
    copy = pltpu.make_async_copy(pattern_hbm, pattern, sem.at[0])
    copy.start()
    zeros[...] = jnp.zeros_like(zeros)
    copy.wait()
    own_places = [places(pattern, q, r) for q in range(2)]
    other_places = [places(pattern, q, c) for q in range(2)]

    def strip_rows(i):
        return pl.ds(i * BS, BS)

    empty = [(own_places[0][1][i] == PMAX) & (own_places[1][1][i] == PMAX) for i in range(TR)]
    for i in range(TR):
        @pl.when(empty[i])
        def _():
            pltpu.make_async_copy(trail.at[strip_rows(i)], updated_hbm.at[strip_rows(i)], sem.at[1 + i]).start()
    for q in range(2):
        for i in range(TR):
            rank = own_places[q][1][i]

            @pl.when(rank < PMAX)
            def _():
                pltpu.make_async_copy(own.at[q, rank], factor_hbm.at[q, i], sem.at[9 + q * TR + i]).start()

            @pl.when(rank == PMAX)
            def _():
                pltpu.make_async_copy(zeros, factor_hbm.at[q, i], sem.at[9 + q * TR + i]).start()
    for q in range(2):
        product = dot_t(own[q].reshape(PMAX * BS, W), other[q].reshape(PMAX * BS, W))
        for a in range(PMAX):
            for b in range(PMAX):
                products[q, a, b] = product[a * BS:(a + 1) * BS, b * BS:(b + 1) * BS]
        for a in range(PMAX + 1):
            products[q, a, PMAX] = jnp.zeros((BS, BS), F32)
            products[q, PMAX, a] = jnp.zeros((BS, BS), F32)
    for i in range(TR):
        @pl.when(jnp.logical_not(empty[i]))
        def _():
            for j in range(TR):
                cols = pl.ds(j * BS, BS)
                strip[strip_rows(i), cols] = trail[strip_rows(i), cols] - (
                    products[0, own_places[0][1][i], other_places[0][1][j]]
                    + products[1, own_places[1][1][i], other_places[1][1][j]]
                )
            pltpu.make_async_copy(strip.at[strip_rows(i)], updated_hbm.at[strip_rows(i)], sem.at[1 + i]).start()
    for i in range(TR):
        pltpu.make_async_copy(strip.at[strip_rows(i)], updated_hbm.at[strip_rows(i)], sem.at[1 + i]).wait()
        for q in range(2):
            pltpu.make_async_copy(zeros, factor_hbm.at[q, i], sem.at[9 + q * TR + i]).wait()


def body(panels, row_pattern, coupling, inverse_factors, trailing):
    hbm = pl.BlockSpec(memory_space=pltpu.HBM)
    pin = lambda x: pltpu.with_memory_space_constraint(x, pltpu.HBM)
    vmem = pl.BlockSpec(memory_space=pltpu.VMEM)
    dma = pltpu.SemaphoreType.DMA
    packed = (2, PMAX, BS, W)
    panels4 = pin(panels.reshape(2, TR, BS, W))
    row_pattern, coupling, inverse_factors, trailing = map(pin, (row_pattern, coupling, inverse_factors, trailing))
    own, other, trail = pl.pallas_call(
        exchange,
        out_shape=(
            jax.ShapeDtypeStruct(packed, BF),
            jax.ShapeDtypeStruct(packed, BF),
            jax.ShapeDtypeStruct(trailing.shape, F32),
        ),
        in_specs=[hbm] * 5,
        out_specs=(vmem, vmem, vmem),
        scratch_shapes=[
            pltpu.SMEM((2, 128), jnp.int32),
            pltpu.VMEM((2, TR, 16, 256), BF),
            pltpu.VMEM((2, PMAX, 16, 256), BF),
            pltpu.VMEM((2, TR, BS, W), BF),
            pltpu.VMEM((2, W, W), BF),
            pltpu.VMEM((W, W), BF),
            pltpu.VMEM((W, W), BF),
            pltpu.VMEM(packed, BF),
            pltpu.VMEM((PMAX + 1, BS, W), BF),
            pltpu.VMEM(packed, BF),
            dma((6,)), dma((8,)), dma((8,)), dma((8,)), dma((8,)), dma((8,)), dma((8,)), dma((8,)), dma((8,)), dma((2,)),
        ],
        compiler_params=pltpu.CompilerParams(collective_id=0, has_side_effects=True, vmem_limit_bytes=40 << 20),
        cost_estimate=pl.CostEstimate(flops=4_000_000_000, bytes_accessed=12 << 20, transcendentals=0),
    )(row_pattern, panels4, coupling, inverse_factors, trailing)
    factor, updated = pl.pallas_call(
        finish,
        out_shape=(
            jax.ShapeDtypeStruct((2, TR, BS, W), BF),
            jax.ShapeDtypeStruct(trailing.shape, F32),
        ),
        in_specs=[hbm, vmem, vmem, vmem],
        out_specs=(hbm, hbm),
        scratch_shapes=[
            pltpu.SMEM((2, 128), jnp.int32),
            pltpu.VMEM((BS, W), BF),
            pltpu.VMEM((2, PMAX + 1, PMAX + 1, BS, BS), F32),
            pltpu.VMEM((TR * BS, TR * BS), F32),
            dma((32,)),
        ],
        compiler_params=pltpu.CompilerParams(vmem_limit_bytes=40 << 20),
    )(row_pattern, own, other, trail)
    return factor.reshape(panels.shape), updated


def solution(mesh):
    placed = (P(None, "row", None), P(), P("row", None), P(), P("row", "col"))
    return jax.shard_map(
        body,
        mesh=mesh,
        in_specs=placed,
        out_specs=(P(None, "row", None), P("row", "col")),
        check_vma=False,
    )
```

```python
import jax
import jax.numpy as jnp
from jax import lax
from jax.experimental import pallas as pl
from jax.experimental.pallas import tpu as pltpu
from jax.sharding import PartitionSpec as P

W = 512
BS = 128
TR = 8
PMAX = 3
NZ = 8
NP = 16
NX = 4
MESH = pl.DeviceIdType.MESH
BF = jnp.bfloat16
F32 = jnp.float32


def dot_t(a, b):
    return lax.dot_general(a, b, (((1,), (1,)), ((), ())), preferred_element_type=F32)


def places(pattern, panel, block):
    tiles = [jnp.int32(0)] * PMAX
    ranks = []
    count = jnp.int32(0)
    for i in range(TR):
        bit = pattern[panel, block * TR + i]
        for j in range(min(i + 1, PMAX)):
            tiles[j] = jnp.where((bit == 1) & (count == j), i, tiles[j])
        ranks.append(jnp.where(bit == 1, count, PMAX))
        count = count + bit
    return tiles, ranks, count


def pick(ranks, tile):
    rank = jnp.int32(PMAX)
    for i in range(TR):
        rank = jnp.where(tile == i, ranks[i], rank)
    return rank


def second_of(panel_one, gathered_first, coupled, inverse):
    held = panel_one.astype(F32) - dot_t(gathered_first, coupled)
    high = held.astype(BF)
    low = (held - high.astype(F32)).astype(BF)
    return dot_t(high, inverse) + dot_t(low, inverse)


def exchange(
    pattern_hbm, panels_hbm, coupling_hbm, inverse_hbm, trailing_hbm,
    own_ref, other_ref, trail_ref,
    pattern, cand, sendbuf, panv, inv, coup, coupled, dland, first, picked,
    local_sem, bsend, brecv, xsend, xrecv, fsend, frecv, dsend, drecv, gsend, grecv, wsem,
):
    r = lax.axis_index("row")
    c = lax.axis_index("col")
    z, k = r // 2, r % 2
    x, y = c // 4, c % 4
    zc = c // 2
    sibling = (z * 2 + 1 - k, c)
    half = c % 2

    def remote(src, dst, send, recv, device):
        return pltpu.make_async_remote_copy(
            src_ref=src, dst_ref=dst, send_sem=send, recv_sem=recv, device_id=device, device_id_type=MESH)

    def across(d):
        return lax.rem(x + d, NX)

    barrier = pltpu.get_barrier_semaphore()

    def greet(device):
        pl.semaphore_signal(barrier, inc=1, device_id=device, device_id_type=MESH)

    greet(sibling)
    for i in range(1, NZ):
        greet((lax.rem(z + i, NZ) * 2 + k, c))
    for d in range(1, NX):
        greet((r, across(d) * 4 + y))

    @pl.when(z != zc)
    def _():
        for i in range(NP // 2):
            greet((c, 2 * i + k))

    piece_rows = pl.ds(pl.multiple_of(16 * (c // 2), 16), 16)
    piece_cols = pl.ds(pl.multiple_of(256 * half, 256), 256)

    def quarter(d):
        return pl.ds(pl.multiple_of(128 * across(d), 128), 128)

    local = [
        pltpu.make_async_copy(pattern_hbm, pattern, local_sem.at[0]),
        pltpu.make_async_copy(panels_hbm.at[:, :, piece_rows, piece_cols], cand, local_sem.at[1]),
        pltpu.make_async_copy(coupling_hbm.at[:, quarter(0)], coup.at[z, k, :, quarter(0)], local_sem.at[2]),
        pltpu.make_async_copy(panels_hbm, panv, local_sem.at[3]),
        pltpu.make_async_copy(inverse_hbm, inv, local_sem.at[4]),
        pltpu.make_async_copy(trailing_hbm, trail_ref, local_sem.at[5]),
    ]
    for copy in local:
        copy.start()
    pl.semaphore_wait(barrier, 2 * NZ - 1 + NX - 1)

    def shard(plane):
        return remote(
            coupling_hbm.at[:, quarter(0)], coup.at[z, k, :, quarter(0)],
            bsend.at[plane], brecv.at[z], (plane * 2 + k, c))

    def shard_from(plane):
        return remote(
            coupling_hbm.at[:, quarter(0)], coup.at[plane, k, :, quarter(0)],
            bsend.at[plane], brecv.at[plane], (plane * 2 + k, c))

    for plane in range(NZ):
        @pl.when(plane != z)
        def _():
            shard(plane).start()

    local[0].wait()
    local[1].wait()
    own_places = [places(pattern, q, r) for q in range(2)]
    for q in range(2):
        tiles, _, count = own_places[q]
        for j in range(PMAX):
            value = cand[q, tiles[j]]
            sendbuf[q, j] = jnp.where(count > j, value, jnp.zeros_like(value))

    def piece(plane):
        return remote(
            sendbuf, dland.at[:, :, piece_rows, piece_cols],
            dsend.at[plane], drecv.at[c // 2], (plane * 2 + half, r))

    for d in [1, 7, 2, 6, 3, 5, 4]:
        piece(lax.rem(z + d, NZ)).start()

    local[3].wait()
    for q in range(2):
        tiles, _, count = own_places[q]
        for j in range(PMAX):
            value = panv[q, tiles[j]]
            picked[q, j] = jnp.where(count > j, value, jnp.zeros_like(value))
    whole = remote(picked, dland, wsem.at[0], wsem.at[1], sibling)

    @pl.when(r == c)
    def _():
        whole.start()
        dland[...] = picked[...]

    local[4].wait()
    first[PMAX] = jnp.zeros((BS, W), BF)
    own_first = dot_t(picked[0].reshape(PMAX * BS, W), inv[0]).astype(BF).reshape(PMAX, BS, W)
    first[:PMAX] = own_first
    own_ref[0] = own_first

    local[2].wait()
    for plane in range(NZ):
        @pl.when(plane != z)
        def _():
            shard_from(plane).wait_recv()

    def quarter_block(d, core):
        return coup.at[:, core, :, quarter(d)]

    def along(d):
        return remote(
            quarter_block(0, k), quarter_block(0, k), xsend.at[d], xrecv.at[NX - d], (r, across(d) * 4 + y))

    def quarter_forward(d, core):
        return remote(
            quarter_block(d, core), quarter_block(d, core), fsend.at[d], frecv.at[d], sibling)

    for d in range(1, NX):
        along(d).start()
    quarter_forward(0, k).start()
    for d in range(1, NX):
        remote(quarter_block(d, k), quarter_block(d, k), xsend.at[d], xrecv.at[d], sibling).wait_recv()
        quarter_forward(d, k).start()

    def piece_at(i, core):
        return dland.at[:, :, pl.ds(16 * i, 16), pl.ds(pl.multiple_of(256 * core, 256), 256)]

    def piece_forward(i, core):
        return remote(piece_at(i, core), piece_at(i, core), gsend.at[i], grecv.at[i], sibling)

    @pl.when(z != zc)
    def _():
        for i in range(NP // 2):
            remote(sendbuf, piece_at(i, k), dsend.at[0], drecv.at[i], sibling).wait_recv()
            piece_forward(i, k).start()

    for d in range(NX):
        quarter_forward(d, 1 - k).wait_recv()
    coupled[...] = dot_t(coup[...].reshape(W, W), inv[0]).astype(BF)

    def matching_first(of_places):
        count = of_places[1][2]
        parts = []
        for j in range(PMAX):
            value = first[pick(of_places[0][1], of_places[1][0][j])]
            parts.append(jnp.where(count > j, value, jnp.zeros_like(value)))
        return jnp.concatenate(parts, axis=0)

    own_ref[1] = second_of(
        picked[1].reshape(PMAX * BS, W), matching_first(own_places), coupled[...], inv[1]
    ).astype(BF).reshape(PMAX, BS, W)

    @pl.when(z != zc)
    def _():
        for i in range(NP // 2):
            piece_forward(i, 1 - k).wait_recv()

    @pl.when((z == zc) & (r != c))
    def _():
        whole.wait_recv()

    other_places = [places(pattern, q, c) for q in range(2)]
    other_first = dot_t(dland[0].reshape(PMAX * BS, W), inv[0]).astype(BF).reshape(PMAX, BS, W)
    first[:PMAX] = other_first
    other_ref[0] = other_first
    other_ref[1] = second_of(
        dland[1].reshape(PMAX * BS, W), matching_first(other_places), coupled[...], inv[1]
    ).astype(BF).reshape(PMAX, BS, W)

    local[5].wait()
    for plane in range(NZ):
        @pl.when(plane != z)
        def _():
            shard(plane).wait_send()
            piece(plane).wait_send()
    for d in range(1, NX):
        along(d).wait_send()
    for d in range(NX):
        quarter_forward(d, k).wait_send()

    @pl.when(z != zc)
    def _():
        for i in range(NP // 2):
            piece_forward(i, k).wait_send()

    @pl.when(r == c)
    def _():
        whole.wait_send()


def finish(pattern_hbm, own, other, trail, factor_hbm, updated_hbm, pattern, zeros, products, strip, sem):
    r = lax.axis_index("row")
    c = lax.axis_index("col")
    copy = pltpu.make_async_copy(pattern_hbm, pattern, sem.at[0])
    copy.start()
    zeros[...] = jnp.zeros_like(zeros)
    copy.wait()
    own_places = [places(pattern, q, r) for q in range(2)]
    other_places = [places(pattern, q, c) for q in range(2)]

    def strip_rows(i):
        return pl.ds(i * BS, BS)

    empty = [(own_places[0][1][i] == PMAX) & (own_places[1][1][i] == PMAX) for i in range(TR)]
    for i in range(TR):
        @pl.when(empty[i])
        def _():
            pltpu.make_async_copy(trail.at[strip_rows(i)], updated_hbm.at[strip_rows(i)], sem.at[1 + i]).start()
    for q in range(2):
        for i in range(TR):
            rank = own_places[q][1][i]

            @pl.when(rank < PMAX)
            def _():
                pltpu.make_async_copy(own.at[q, rank], factor_hbm.at[q, i], sem.at[9 + q * TR + i]).start()

            @pl.when(rank == PMAX)
            def _():
                pltpu.make_async_copy(zeros, factor_hbm.at[q, i], sem.at[9 + q * TR + i]).start()
    for q in range(2):
        product = dot_t(own[q].reshape(PMAX * BS, W), other[q].reshape(PMAX * BS, W))
        for a in range(PMAX):
            for b in range(PMAX):
                products[q, a, b] = product[a * BS:(a + 1) * BS, b * BS:(b + 1) * BS]
        for a in range(PMAX + 1):
            products[q, a, PMAX] = jnp.zeros((BS, BS), F32)
            products[q, PMAX, a] = jnp.zeros((BS, BS), F32)
    for i in range(TR):
        @pl.when(jnp.logical_not(empty[i]))
        def _():
            for j in range(TR):
                cols = pl.ds(j * BS, BS)
                strip[strip_rows(i), cols] = trail[strip_rows(i), cols] - (
                    products[0, own_places[0][1][i], other_places[0][1][j]]
                    + products[1, own_places[1][1][i], other_places[1][1][j]]
                )
            pltpu.make_async_copy(strip.at[strip_rows(i)], updated_hbm.at[strip_rows(i)], sem.at[1 + i]).start()
    for i in range(TR):
        pltpu.make_async_copy(strip.at[strip_rows(i)], updated_hbm.at[strip_rows(i)], sem.at[1 + i]).wait()
        for q in range(2):
            pltpu.make_async_copy(zeros, factor_hbm.at[q, i], sem.at[9 + q * TR + i]).wait()


def body(panels, row_pattern, coupling, inverse_factors, trailing):
    hbm = pl.BlockSpec(memory_space=pltpu.HBM)
    pin = lambda x: pltpu.with_memory_space_constraint(x, pltpu.HBM)
    vmem = pl.BlockSpec(memory_space=pltpu.VMEM)
    dma = pltpu.SemaphoreType.DMA
    packed = (2, PMAX, BS, W)
    panels4 = pin(panels.reshape(2, TR, BS, W))
    row_pattern, coupling, inverse_factors, trailing = map(pin, (row_pattern, coupling, inverse_factors, trailing))
    own, other, trail = pl.pallas_call(
        exchange,
        out_shape=(
            jax.ShapeDtypeStruct(packed, BF),
            jax.ShapeDtypeStruct(packed, BF),
            jax.ShapeDtypeStruct(trailing.shape, F32),
        ),
        in_specs=[hbm] * 5,
        out_specs=(vmem, vmem, vmem),
        scratch_shapes=[
            pltpu.SMEM((2, 128), jnp.int32),
            pltpu.VMEM((2, TR, 16, 256), BF),
            pltpu.VMEM((2, PMAX, 16, 256), BF),
            pltpu.VMEM((2, TR, BS, W), BF),
            pltpu.VMEM((2, W, W), BF),
            pltpu.VMEM((NZ, 2, 32, W), BF),
            pltpu.VMEM((W, W), BF),
            pltpu.VMEM(packed, BF),
            pltpu.VMEM((PMAX + 1, BS, W), BF),
            pltpu.VMEM(packed, BF),
            dma((6,)), dma((NZ,)), dma((NZ,)), dma((NX,)), dma((NX,)), dma((NX,)), dma((NX,)),
            dma((NZ,)), dma((NP // 2,)), dma((NP // 2,)), dma((NP // 2,)), dma((2,)),
        ],
        compiler_params=pltpu.CompilerParams(collective_id=0, has_side_effects=True, vmem_limit_bytes=40 << 20),
        cost_estimate=pl.CostEstimate(flops=4_000_000_000, bytes_accessed=12 << 20, transcendentals=0),
    )(row_pattern, panels4, coupling, inverse_factors, trailing)
    factor, updated = pl.pallas_call(
        finish,
        out_shape=(
            jax.ShapeDtypeStruct((2, TR, BS, W), BF),
            jax.ShapeDtypeStruct(trailing.shape, F32),
        ),
        in_specs=[hbm, vmem, vmem, vmem],
        out_specs=(hbm, hbm),
        scratch_shapes=[
            pltpu.SMEM((2, 128), jnp.int32),
            pltpu.VMEM((BS, W), BF),
            pltpu.VMEM((2, PMAX + 1, PMAX + 1, BS, BS), F32),
            pltpu.VMEM((TR * BS, TR * BS), F32),
            dma((32,)),
        ],
        compiler_params=pltpu.CompilerParams(vmem_limit_bytes=40 << 20),
    )(row_pattern, own, other, trail)
    return factor.reshape(panels.shape), updated


def solution(mesh):
    placed = (P(None, "row", None), P(), P("row", None), P(), P("row", "col"))
    return jax.shard_map(
        body,
        mesh=mesh,
        in_specs=placed,
        out_specs=(P(None, "row", None), P("row", "col")),
        check_vma=False,
    )
```

```python
import jax
import jax.numpy as jnp
from jax import lax
from jax.experimental import pallas as pl
from jax.experimental.pallas import tpu as pltpu
from jax.sharding import PartitionSpec as P

W = 512
BS = 128
TR = 8
PMAX = 3
NZ = 8
NP = 16
NX = 4
MESH = pl.DeviceIdType.MESH
BF = jnp.bfloat16
F32 = jnp.float32


def dot_t(a, b):
    return lax.dot_general(a, b, (((1,), (1,)), ((), ())), preferred_element_type=F32)


def places(pattern, panel, block):
    tiles = [jnp.int32(0)] * PMAX
    ranks = []
    count = jnp.int32(0)
    for i in range(TR):
        bit = pattern[panel, block * TR + i]
        for j in range(min(i + 1, PMAX)):
            tiles[j] = jnp.where((bit == 1) & (count == j), i, tiles[j])
        ranks.append(jnp.where(bit == 1, count, PMAX))
        count = count + bit
    return tiles, ranks, count


def pick(ranks, tile):
    rank = jnp.int32(PMAX)
    for i in range(TR):
        rank = jnp.where(tile == i, ranks[i], rank)
    return rank


def second_of(panel_one, gathered_first, coupled, inverse):
    held = panel_one.astype(F32) - dot_t(gathered_first, coupled)
    high = held.astype(BF)
    low = (held - high.astype(F32)).astype(BF)
    return dot_t(high, inverse) + dot_t(low, inverse)


def exchange(
    pattern_hbm, panels_hbm, coupling_hbm, inverse_hbm, trailing_hbm,
    own_ref, other_ref, trail_ref,
    pattern, cand, sendbuf, panv, inv, coup, coupled, dland, first, picked,
    local_sem, bsend, brecv, xsend, xrecv, fsend, frecv, dsend, drecv, gsend, grecv, wsem, ready,
):
    r = lax.axis_index("row")
    c = lax.axis_index("col")
    z, k = r // 2, r % 2
    x, y = c // 4, c % 4
    zc = c // 2
    sibling = (z * 2 + 1 - k, c)
    half = c % 2

    def remote(src, dst, send, recv, device):
        return pltpu.make_async_remote_copy(
            src_ref=src, dst_ref=dst, send_sem=send, recv_sem=recv, device_id=device, device_id_type=MESH)

    def across(d):
        return lax.rem(x + d, NX)

    barrier = pltpu.get_barrier_semaphore()

    def greet(device):
        pl.semaphore_signal(barrier, inc=1, device_id=device, device_id_type=MESH)

    greet(sibling)
    for i in range(1, NZ):
        greet((lax.rem(z + i, NZ) * 2 + k, c))
    for d in range(1, NX):
        greet((r, across(d) * 4 + y))

    @pl.when(r != c)
    def _():
        greet((z * 2 + half, r))

    piece_rows = pl.ds(pl.multiple_of(16 * (c // 2), 16), 16)
    piece_cols = pl.ds(pl.multiple_of(256 * half, 256), 256)

    def quarter(d):
        return pl.ds(pl.multiple_of(128 * across(d), 128), 128)

    local = [
        pltpu.make_async_copy(pattern_hbm, pattern, local_sem.at[0]),
        pltpu.make_async_copy(panels_hbm.at[:, :, piece_rows, piece_cols], cand, local_sem.at[1]),
        pltpu.make_async_copy(coupling_hbm.at[:, quarter(0)], coup.at[z, k, :, quarter(0)], local_sem.at[2]),
        pltpu.make_async_copy(panels_hbm, panv, local_sem.at[3]),
        pltpu.make_async_copy(inverse_hbm, inv, local_sem.at[4]),
        pltpu.make_async_copy(trailing_hbm, trail_ref, local_sem.at[5]),
    ]
    for copy in local:
        copy.start()
    near = NZ - 1 + 1 + NX - 1
    teller = z == zc

    @pl.when(jnp.logical_not(teller))
    def _():
        pl.semaphore_wait(barrier, near)

    @pl.when(teller & (r != c))
    def _():
        pl.semaphore_wait(barrier, near + NP // 2)

    @pl.when(r == c)
    def _():
        pl.semaphore_wait(barrier, near + NP // 2 - 1)


    for i in range(NP // 2):
        @pl.when(teller & ((r != c) | (2 * i + k != c)))
        def _():
            pl.semaphore_signal(ready, inc=1, device_id=(c, 2 * i + k), device_id_type=MESH)

    def shard(plane):
        return remote(
            coupling_hbm.at[:, quarter(0)], coup.at[z, k, :, quarter(0)],
            bsend.at[plane], brecv.at[z], (plane * 2 + k, c))

    def shard_from(plane):
        return remote(
            coupling_hbm.at[:, quarter(0)], coup.at[plane, k, :, quarter(0)],
            bsend.at[plane], brecv.at[plane], (plane * 2 + k, c))

    for plane in range(NZ):
        @pl.when(plane != z)
        def _():
            shard(plane).start()

    local[0].wait()
    local[1].wait()
    own_places = [places(pattern, q, r) for q in range(2)]
    for q in range(2):
        tiles, _, count = own_places[q]
        for j in range(PMAX):
            value = cand[q, tiles[j]]
            sendbuf[q, j] = jnp.where(count > j, value, jnp.zeros_like(value))

    def piece(plane):
        return remote(
            sendbuf, dland.at[:, :, piece_rows, piece_cols],
            dsend.at[plane], drecv.at[c // 2], (plane * 2 + half, r))

    @pl.when(r != c)
    def _():
        pl.semaphore_wait(ready, 1)

    for plane in range(4):
        @pl.when(z >= 4)
        def _():
            piece(plane).start()

    for d in [1, 7, 2, 6, 3, 5, 4]:
        @pl.when((z < 4) | (lax.rem(z + d, NZ) >= 4))
        def _():
            piece(lax.rem(z + d, NZ)).start()


    local[3].wait()
    for q in range(2):
        tiles, _, count = own_places[q]
        for j in range(PMAX):
            value = panv[q, tiles[j]]
            picked[q, j] = jnp.where(count > j, value, jnp.zeros_like(value))
    whole = remote(picked, dland, wsem.at[0], wsem.at[1], sibling)

    @pl.when(r == c)
    def _():
        whole.start()
        dland[...] = picked[...]

    local[2].wait()
    for plane in range(NZ):
        @pl.when(plane != z)
        def _():
            shard_from(plane).wait_recv()

    def quarter_block(d, core):
        return coup.at[:, core, :, quarter(d)]

    def along(d):
        return remote(
            quarter_block(0, k), quarter_block(0, k), xsend.at[d], xrecv.at[NX - d], (r, across(d) * 4 + y))

    def quarter_forward(d, core):
        return remote(
            quarter_block(d, core), quarter_block(d, core), fsend.at[d], frecv.at[d], sibling)

    for d in range(1, NX):
        along(d).start()
    quarter_forward(0, k).start()
    local[4].wait()
    first[PMAX] = jnp.zeros((BS, W), BF)
    own_first = dot_t(picked[0].reshape(PMAX * BS, W), inv[0]).astype(BF).reshape(PMAX, BS, W)
    first[:PMAX] = own_first
    own_ref[0] = own_first

    for d in range(1, NX):
        remote(quarter_block(d, k), quarter_block(d, k), xsend.at[d], xrecv.at[d], sibling).wait_recv()
        quarter_forward(d, k).start()

    def piece_at(i, core):
        return dland.at[:, :, pl.ds(16 * i, 16), pl.ds(pl.multiple_of(256 * core, 256), 256)]

    def piece_forward(i, core):
        return remote(piece_at(i, core), piece_at(i, core), gsend.at[i], grecv.at[i], sibling)

    @pl.when(z != zc)
    def _():
        for i in range(NP // 2):
            remote(sendbuf, piece_at(i, k), dsend.at[0], drecv.at[i], sibling).wait_recv()
            piece_forward(i, k).start()

    for d in range(NX):
        quarter_forward(d, 1 - k).wait_recv()
    coupled[...] = dot_t(coup[...].reshape(W, W), inv[0]).astype(BF)

    def matching_first(of_places):
        count = of_places[1][2]
        parts = []
        for j in range(PMAX):
            value = first[pick(of_places[0][1], of_places[1][0][j])]
            parts.append(jnp.where(count > j, value, jnp.zeros_like(value)))
        return jnp.concatenate(parts, axis=0)

    own_ref[1] = second_of(
        picked[1].reshape(PMAX * BS, W), matching_first(own_places), coupled[...], inv[1]
    ).astype(BF).reshape(PMAX, BS, W)

    @pl.when(z != zc)
    def _():
        for i in range(NP // 2):
            piece_forward(i, 1 - k).wait_recv()

    @pl.when((z == zc) & (r != c))
    def _():
        whole.wait_recv()

    other_places = [places(pattern, q, c) for q in range(2)]
    other_first = dot_t(dland[0].reshape(PMAX * BS, W), inv[0]).astype(BF).reshape(PMAX, BS, W)
    first[:PMAX] = other_first
    other_ref[0] = other_first
    other_ref[1] = second_of(
        dland[1].reshape(PMAX * BS, W), matching_first(other_places), coupled[...], inv[1]
    ).astype(BF).reshape(PMAX, BS, W)

    local[5].wait()
    for plane in range(NZ):
        @pl.when(plane != z)
        def _():
            shard(plane).wait_send()
            piece(plane).wait_send()
    for d in range(1, NX):
        along(d).wait_send()
    for d in range(NX):
        quarter_forward(d, k).wait_send()

    @pl.when(z != zc)
    def _():
        for i in range(NP // 2):
            piece_forward(i, k).wait_send()

    @pl.when(r == c)
    def _():
        whole.wait_send()


def finish(pattern_hbm, own, other, trail, factor_hbm, updated_hbm, pattern, zeros, products, strip, sem):
    r = lax.axis_index("row")
    c = lax.axis_index("col")
    copy = pltpu.make_async_copy(pattern_hbm, pattern, sem.at[0])
    copy.start()
    zeros[...] = jnp.zeros_like(zeros)
    copy.wait()
    own_places = [places(pattern, q, r) for q in range(2)]
    other_places = [places(pattern, q, c) for q in range(2)]

    def strip_rows(i):
        return pl.ds(i * BS, BS)

    empty = [(own_places[0][1][i] == PMAX) & (own_places[1][1][i] == PMAX) for i in range(TR)]
    for i in range(TR):
        @pl.when(empty[i])
        def _():
            pltpu.make_async_copy(trail.at[strip_rows(i)], updated_hbm.at[strip_rows(i)], sem.at[1 + i]).start()
    for q in range(2):
        for i in range(TR):
            rank = own_places[q][1][i]

            @pl.when(rank < PMAX)
            def _():
                pltpu.make_async_copy(own.at[q, rank], factor_hbm.at[q, i], sem.at[9 + q * TR + i]).start()

            @pl.when(rank == PMAX)
            def _():
                pltpu.make_async_copy(zeros, factor_hbm.at[q, i], sem.at[9 + q * TR + i]).start()
    for q in range(2):
        product = dot_t(own[q].reshape(PMAX * BS, W), other[q].reshape(PMAX * BS, W))
        for a in range(PMAX):
            for b in range(PMAX):
                products[q, a, b] = product[a * BS:(a + 1) * BS, b * BS:(b + 1) * BS]
        for a in range(PMAX + 1):
            products[q, a, PMAX] = jnp.zeros((BS, BS), F32)
            products[q, PMAX, a] = jnp.zeros((BS, BS), F32)
    for i in range(TR):
        @pl.when(jnp.logical_not(empty[i]))
        def _():
            for j in range(TR):
                cols = pl.ds(j * BS, BS)
                strip[strip_rows(i), cols] = trail[strip_rows(i), cols] - (
                    products[0, own_places[0][1][i], other_places[0][1][j]]
                    + products[1, own_places[1][1][i], other_places[1][1][j]]
                )
            pltpu.make_async_copy(strip.at[strip_rows(i)], updated_hbm.at[strip_rows(i)], sem.at[1 + i]).start()
    for i in range(TR):
        pltpu.make_async_copy(strip.at[strip_rows(i)], updated_hbm.at[strip_rows(i)], sem.at[1 + i]).wait()
        for q in range(2):
            pltpu.make_async_copy(zeros, factor_hbm.at[q, i], sem.at[9 + q * TR + i]).wait()


def body(panels, row_pattern, coupling, inverse_factors, trailing):
    hbm = pl.BlockSpec(memory_space=pltpu.HBM)
    pin = lambda x: pltpu.with_memory_space_constraint(x, pltpu.HBM)
    vmem = pl.BlockSpec(memory_space=pltpu.VMEM)
    dma = pltpu.SemaphoreType.DMA
    packed = (2, PMAX, BS, W)
    panels4 = pin(panels.reshape(2, TR, BS, W))
    row_pattern, coupling, inverse_factors, trailing = map(pin, (row_pattern, coupling, inverse_factors, trailing))
    own, other, trail = pl.pallas_call(
        exchange,
        out_shape=(
            jax.ShapeDtypeStruct(packed, BF),
            jax.ShapeDtypeStruct(packed, BF),
            jax.ShapeDtypeStruct(trailing.shape, F32),
        ),
        in_specs=[hbm] * 5,
        out_specs=(vmem, vmem, vmem),
        scratch_shapes=[
            pltpu.SMEM((2, 128), jnp.int32),
            pltpu.VMEM((2, TR, 16, 256), BF),
            pltpu.VMEM((2, PMAX, 16, 256), BF),
            pltpu.VMEM((2, TR, BS, W), BF),
            pltpu.VMEM((2, W, W), BF),
            pltpu.VMEM((NZ, 2, 32, W), BF),
            pltpu.VMEM((W, W), BF),
            pltpu.VMEM(packed, BF),
            pltpu.VMEM((PMAX + 1, BS, W), BF),
            pltpu.VMEM(packed, BF),
            dma((6,)), dma((NZ,)), dma((NZ,)), dma((NX,)), dma((NX,)), dma((NX,)), dma((NX,)),
            dma((NZ,)), dma((NP // 2,)), dma((NP // 2,)), dma((NP // 2,)), dma((2,)), pltpu.SemaphoreType.REGULAR,
        ],
        compiler_params=pltpu.CompilerParams(collective_id=0, has_side_effects=True, vmem_limit_bytes=40 << 20),
        cost_estimate=pl.CostEstimate(flops=4_000_000_000, bytes_accessed=12 << 20, transcendentals=0),
    )(row_pattern, panels4, coupling, inverse_factors, trailing)
    factor, updated = pl.pallas_call(
        finish,
        out_shape=(
            jax.ShapeDtypeStruct((2, TR, BS, W), BF),
            jax.ShapeDtypeStruct(trailing.shape, F32),
        ),
        in_specs=[hbm, vmem, vmem, vmem],
        out_specs=(hbm, hbm),
        scratch_shapes=[
            pltpu.SMEM((2, 128), jnp.int32),
            pltpu.VMEM((BS, W), BF),
            pltpu.VMEM((2, PMAX + 1, PMAX + 1, BS, BS), F32),
            pltpu.VMEM((TR * BS, TR * BS), F32),
            dma((32,)),
        ],
        compiler_params=pltpu.CompilerParams(vmem_limit_bytes=40 << 20),
    )(row_pattern, own, other, trail)
    return factor.reshape(panels.shape), updated


def solution(mesh):
    placed = (P(None, "row", None), P(), P("row", None), P(), P("row", "col"))
    return jax.shard_map(
        body,
        mesh=mesh,
        in_specs=placed,
        out_specs=(P(None, "row", None), P("row", "col")),
        check_vma=False,
    )
```

```python
import jax
import jax.numpy as jnp
from jax import lax
from jax.experimental import pallas as pl
from jax.experimental.pallas import tpu as pltpu
from jax.sharding import PartitionSpec as P

W = 512
BS = 128
TR = 8
PMAX = 3
NZ = 8
NP = 16
NX = 4
MESH = pl.DeviceIdType.MESH
BF = jnp.bfloat16
F32 = jnp.float32


def dot_t(a, b):
    return lax.dot_general(a, b, (((1,), (1,)), ((), ())), preferred_element_type=F32)


def places(pattern, panel, block):
    tiles = [jnp.int32(0)] * PMAX
    ranks = []
    count = jnp.int32(0)
    for i in range(TR):
        bit = pattern[panel, block * TR + i]
        for j in range(min(i + 1, PMAX)):
            tiles[j] = jnp.where((bit == 1) & (count == j), i, tiles[j])
        ranks.append(jnp.where(bit == 1, count, PMAX))
        count = count + bit
    return tiles, ranks, count


def pick(ranks, tile):
    rank = jnp.int32(PMAX)
    for i in range(TR):
        rank = jnp.where(tile == i, ranks[i], rank)
    return rank


def second_of(panel_one, gathered_first, coupled, inverse):
    held = panel_one.astype(F32) - dot_t(gathered_first, coupled)
    high = held.astype(BF)
    low = (held - high.astype(F32)).astype(BF)
    return dot_t(high, inverse) + dot_t(low, inverse)


def exchange(
    pattern_hbm, panels_hbm, coupling_hbm, inverse_hbm, trailing_hbm,
    own_ref, other_ref, trail_ref,
    pattern, cand, sendbuf, panv, inv, coup, coupled, dland, first, picked,
    local_sem, bsend, brecv, xsend, xrecv, fsend, frecv, dsend, drecv, gsend, grecv, wsem, ready,
):
    r = lax.axis_index("row")
    c = lax.axis_index("col")
    z, k = r // 2, r % 2
    x, y = c // 4, c % 4
    zc = c // 2
    sibling = (z * 2 + 1 - k, c)
    half = c % 2

    def remote(src, dst, send, recv, device):
        return pltpu.make_async_remote_copy(
            src_ref=src, dst_ref=dst, send_sem=send, recv_sem=recv, device_id=device, device_id_type=MESH)

    def across(d):
        return lax.rem(x + d, NX)

    barrier = pltpu.get_barrier_semaphore()

    def greet(device):
        pl.semaphore_signal(barrier, inc=1, device_id=device, device_id_type=MESH)

    greet(sibling)
    for i in range(1, NZ):
        greet((lax.rem(z + i, NZ) * 2 + k, c))
    for d in range(1, NX):
        greet((r, across(d) * 4 + y))

    @pl.when(r != c)
    def _():
        greet((z * 2 + half, r))

    piece_rows = pl.ds(pl.multiple_of(16 * (c // 2), 16), 16)
    piece_cols = pl.ds(pl.multiple_of(256 * half, 256), 256)

    def quarter(d):
        return pl.ds(pl.multiple_of(128 * across(d), 128), 128)

    local = [
        pltpu.make_async_copy(pattern_hbm, pattern, local_sem.at[0]),
        pltpu.make_async_copy(panels_hbm.at[:, :, piece_rows, piece_cols], cand, local_sem.at[1]),
        pltpu.make_async_copy(coupling_hbm.at[:, quarter(0)], coup.at[z, k, :, quarter(0)], local_sem.at[2]),
        pltpu.make_async_copy(panels_hbm, panv, local_sem.at[3]),
        pltpu.make_async_copy(inverse_hbm, inv, local_sem.at[4]),
        pltpu.make_async_copy(trailing_hbm, trail_ref, local_sem.at[5]),
    ]
    for copy in local:
        copy.start()
    near = NZ - 1 + 1 + NX - 1
    teller = z == zc

    @pl.when(jnp.logical_not(teller))
    def _():
        pl.semaphore_wait(barrier, near)

    @pl.when(teller & (r != c))
    def _():
        pl.semaphore_wait(barrier, near + NP // 2)

    @pl.when(r == c)
    def _():
        pl.semaphore_wait(barrier, near + NP // 2 - 1)


    for i in range(NP // 2):
        @pl.when(teller & ((r != c) | (2 * i + k != c)))
        def _():
            pl.semaphore_signal(ready, inc=1, device_id=(c, 2 * i + k), device_id_type=MESH)

    def shard(plane):
        return remote(
            coupling_hbm.at[:, quarter(0)], coup.at[z, k, :, quarter(0)],
            bsend.at[plane], brecv.at[z], (plane * 2 + k, c))

    def shard_from(plane):
        return remote(
            coupling_hbm.at[:, quarter(0)], coup.at[plane, k, :, quarter(0)],
            bsend.at[plane], brecv.at[plane], (plane * 2 + k, c))

    for plane in range(NZ):
        @pl.when(plane != z)
        def _():
            shard(plane).start()

    local[0].wait()
    local[1].wait()
    own_places = [places(pattern, q, r) for q in range(2)]
    for q in range(2):
        tiles, _, count = own_places[q]
        for j in range(PMAX):
            value = cand[q, tiles[j]]
            sendbuf[q, j] = jnp.where(count > j, value, jnp.zeros_like(value))

    def piece(plane):
        return remote(
            sendbuf, dland.at[:, :, piece_rows, piece_cols],
            dsend.at[plane], drecv.at[c // 2], (plane * 2 + half, r))

    @pl.when(r != c)
    def _():
        pl.semaphore_wait(ready, 1)

    for plane in range(4):
        @pl.when(z >= 4)
        def _():
            piece(plane).start()

    for d in [1, 7, 2, 6, 3, 5, 4]:
        @pl.when((z < 4) & (lax.rem(z + d, NZ) < 4))
        def _():
            piece(lax.rem(z + d, NZ)).start()

    for d in [1, 7, 2, 6, 3, 5, 4]:
        @pl.when(lax.rem(z + d, NZ) >= 4)
        def _():
            piece(lax.rem(z + d, NZ)).start()

    local[3].wait()
    for q in range(2):
        tiles, _, count = own_places[q]
        for j in range(PMAX):
            value = panv[q, tiles[j]]
            picked[q, j] = jnp.where(count > j, value, jnp.zeros_like(value))
    whole = remote(picked, dland, wsem.at[0], wsem.at[1], sibling)

    @pl.when(r == c)
    def _():
        whole.start()
        dland[...] = picked[...]

    local[2].wait()
    for plane in range(NZ):
        @pl.when(plane != z)
        def _():
            shard_from(plane).wait_recv()

    def quarter_block(d, core):
        return coup.at[:, core, :, quarter(d)]

    def along(d):
        return remote(
            quarter_block(0, k), quarter_block(0, k), xsend.at[d], xrecv.at[NX - d], (r, across(d) * 4 + y))

    def quarter_forward(d, core):
        return remote(
            quarter_block(d, core), quarter_block(d, core), fsend.at[d], frecv.at[d], sibling)

    for d in range(1, NX):
        along(d).start()
    quarter_forward(0, k).start()
    local[4].wait()
    first[PMAX] = jnp.zeros((BS, W), BF)
    own_first = dot_t(picked[0].reshape(PMAX * BS, W), inv[0]).astype(BF).reshape(PMAX, BS, W)
    first[:PMAX] = own_first
    own_ref[0] = own_first

    for d in range(1, NX):
        remote(quarter_block(d, k), quarter_block(d, k), xsend.at[d], xrecv.at[d], sibling).wait_recv()
        quarter_forward(d, k).start()

    def piece_at(i, core):
        return dland.at[:, :, pl.ds(16 * i, 16), pl.ds(pl.multiple_of(256 * core, 256), 256)]

    def piece_forward(i, core):
        return remote(piece_at(i, core), piece_at(i, core), gsend.at[i], grecv.at[i], sibling)

    @pl.when(z != zc)
    def _():
        for i in range(NP // 2):
            remote(sendbuf, piece_at(i, k), dsend.at[0], drecv.at[i], sibling).wait_recv()
            piece_forward(i, k).start()

    for d in range(NX):
        quarter_forward(d, 1 - k).wait_recv()
    coupled[...] = dot_t(coup[...].reshape(W, W), inv[0]).astype(BF)

    def matching_first(of_places):
        count = of_places[1][2]
        parts = []
        for j in range(PMAX):
            value = first[pick(of_places[0][1], of_places[1][0][j])]
            parts.append(jnp.where(count > j, value, jnp.zeros_like(value)))
        return jnp.concatenate(parts, axis=0)

    own_ref[1] = second_of(
        picked[1].reshape(PMAX * BS, W), matching_first(own_places), coupled[...], inv[1]
    ).astype(BF).reshape(PMAX, BS, W)

    @pl.when(z != zc)
    def _():
        for i in range(NP // 2):
            piece_forward(i, 1 - k).wait_recv()

    @pl.when((z == zc) & (r != c))
    def _():
        whole.wait_recv()

    other_places = [places(pattern, q, c) for q in range(2)]
    other_first = dot_t(dland[0].reshape(PMAX * BS, W), inv[0]).astype(BF).reshape(PMAX, BS, W)
    first[:PMAX] = other_first
    other_ref[0] = other_first
    other_ref[1] = second_of(
        dland[1].reshape(PMAX * BS, W), matching_first(other_places), coupled[...], inv[1]
    ).astype(BF).reshape(PMAX, BS, W)

    local[5].wait()
    for plane in range(NZ):
        @pl.when(plane != z)
        def _():
            shard(plane).wait_send()
            piece(plane).wait_send()
    for d in range(1, NX):
        along(d).wait_send()
    for d in range(NX):
        quarter_forward(d, k).wait_send()

    @pl.when(z != zc)
    def _():
        for i in range(NP // 2):
            piece_forward(i, k).wait_send()

    @pl.when(r == c)
    def _():
        whole.wait_send()


def finish(pattern_hbm, own, other, trail, factor_hbm, updated_hbm, pattern, zeros, products, strip, sem):
    r = lax.axis_index("row")
    c = lax.axis_index("col")
    copy = pltpu.make_async_copy(pattern_hbm, pattern, sem.at[0])
    copy.start()
    zeros[...] = jnp.zeros_like(zeros)
    copy.wait()
    own_places = [places(pattern, q, r) for q in range(2)]
    other_places = [places(pattern, q, c) for q in range(2)]

    def strip_rows(i):
        return pl.ds(i * BS, BS)

    empty = [(own_places[0][1][i] == PMAX) & (own_places[1][1][i] == PMAX) for i in range(TR)]
    for i in range(TR):
        @pl.when(empty[i])
        def _():
            pltpu.make_async_copy(trail.at[strip_rows(i)], updated_hbm.at[strip_rows(i)], sem.at[1 + i]).start()
    for q in range(2):
        for i in range(TR):
            rank = own_places[q][1][i]

            @pl.when(rank < PMAX)
            def _():
                pltpu.make_async_copy(own.at[q, rank], factor_hbm.at[q, i], sem.at[9 + q * TR + i]).start()

            @pl.when(rank == PMAX)
            def _():
                pltpu.make_async_copy(zeros, factor_hbm.at[q, i], sem.at[9 + q * TR + i]).start()
    for q in range(2):
        product = dot_t(own[q].reshape(PMAX * BS, W), other[q].reshape(PMAX * BS, W))
        for a in range(PMAX):
            for b in range(PMAX):
                products[q, a, b] = product[a * BS:(a + 1) * BS, b * BS:(b + 1) * BS]
        for a in range(PMAX + 1):
            products[q, a, PMAX] = jnp.zeros((BS, BS), F32)
            products[q, PMAX, a] = jnp.zeros((BS, BS), F32)
    for i in range(TR):
        @pl.when(jnp.logical_not(empty[i]))
        def _():
            for j in range(TR):
                cols = pl.ds(j * BS, BS)
                strip[strip_rows(i), cols] = trail[strip_rows(i), cols] - (
                    products[0, own_places[0][1][i], other_places[0][1][j]]
                    + products[1, own_places[1][1][i], other_places[1][1][j]]
                )
            pltpu.make_async_copy(strip.at[strip_rows(i)], updated_hbm.at[strip_rows(i)], sem.at[1 + i]).start()
    for i in range(TR):
        pltpu.make_async_copy(strip.at[strip_rows(i)], updated_hbm.at[strip_rows(i)], sem.at[1 + i]).wait()
        for q in range(2):
            pltpu.make_async_copy(zeros, factor_hbm.at[q, i], sem.at[9 + q * TR + i]).wait()


def body(panels, row_pattern, coupling, inverse_factors, trailing):
    hbm = pl.BlockSpec(memory_space=pltpu.HBM)
    pin = lambda x: pltpu.with_memory_space_constraint(x, pltpu.HBM)
    vmem = pl.BlockSpec(memory_space=pltpu.VMEM)
    dma = pltpu.SemaphoreType.DMA
    packed = (2, PMAX, BS, W)
    panels4 = pin(panels.reshape(2, TR, BS, W))
    row_pattern, coupling, inverse_factors, trailing = map(pin, (row_pattern, coupling, inverse_factors, trailing))
    own, other, trail = pl.pallas_call(
        exchange,
        out_shape=(
            jax.ShapeDtypeStruct(packed, BF),
            jax.ShapeDtypeStruct(packed, BF),
            jax.ShapeDtypeStruct(trailing.shape, F32),
        ),
        in_specs=[hbm] * 5,
        out_specs=(vmem, vmem, vmem),
        scratch_shapes=[
            pltpu.SMEM((2, 128), jnp.int32),
            pltpu.VMEM((2, TR, 16, 256), BF),
            pltpu.VMEM((2, PMAX, 16, 256), BF),
            pltpu.VMEM((2, TR, BS, W), BF),
            pltpu.VMEM((2, W, W), BF),
            pltpu.VMEM((NZ, 2, 32, W), BF),
            pltpu.VMEM((W, W), BF),
            pltpu.VMEM(packed, BF),
            pltpu.VMEM((PMAX + 1, BS, W), BF),
            pltpu.VMEM(packed, BF),
            dma((6,)), dma((NZ,)), dma((NZ,)), dma((NX,)), dma((NX,)), dma((NX,)), dma((NX,)),
            dma((NZ,)), dma((NP // 2,)), dma((NP // 2,)), dma((NP // 2,)), dma((2,)), pltpu.SemaphoreType.REGULAR,
        ],
        compiler_params=pltpu.CompilerParams(collective_id=0, has_side_effects=True, vmem_limit_bytes=40 << 20),
        cost_estimate=pl.CostEstimate(flops=4_000_000_000, bytes_accessed=12 << 20, transcendentals=0),
    )(row_pattern, panels4, coupling, inverse_factors, trailing)
    factor, updated = pl.pallas_call(
        finish,
        out_shape=(
            jax.ShapeDtypeStruct((2, TR, BS, W), BF),
            jax.ShapeDtypeStruct(trailing.shape, F32),
        ),
        in_specs=[hbm, vmem, vmem, vmem],
        out_specs=(hbm, hbm),
        scratch_shapes=[
            pltpu.SMEM((2, 128), jnp.int32),
            pltpu.VMEM((BS, W), BF),
            pltpu.VMEM((2, PMAX + 1, PMAX + 1, BS, BS), F32),
            pltpu.VMEM((TR * BS, TR * BS), F32),
            dma((32,)),
        ],
        compiler_params=pltpu.CompilerParams(vmem_limit_bytes=40 << 20),
    )(row_pattern, own, other, trail)
    return factor.reshape(panels.shape), updated


def solution(mesh):
    placed = (P(None, "row", None), P(), P("row", None), P(), P("row", "col"))
    return jax.shard_map(
        body,
        mesh=mesh,
        in_specs=placed,
        out_specs=(P(None, "row", None), P("row", "col")),
        check_vma=False,
    )
```
